256 devices in a mesh: section: 4 (over x), ep: 64 (over y, z, core).
Axes of the slice: x: 4, y: 4, z: 8, core: 2. Of those that a mesh axis runs over, the one named last changes fastest.
Arguments:
- hidden_in: bfloat16 [4, 64, 4096], P(None, 'ep'), may hold values from -4 to 4
- norm_gain: float32 [4, 4096], P('section'), may hold values from 0.1 to 1.9
- gate_weight: bfloat16 [4, 4096, 24576], P('section', None, 'ep'), may hold values from -0.09375 to 0.09375
- up_weight: bfloat16 [4, 4096, 24576], P('section', None, 'ep'), may hold values from -0.09375 to 0.09375
- down_weight: bfloat16 [4, 24576, 4096], P('section', 'ep'), may hold values from -0.15625 to 0.15625
- routes: int32 [4, 4, 64, 8], P('section'), may hold values from 0 to 15, all different within a row; in each aligned block of 64 rows (0 to 63, 64 to 127, ..., all dimensions but the last counted through in order) at most 48 rows name the same one
- route_weight: float32 [4, 4, 64, 8], P('section'), may hold values from 0.2 to 1
Outputs:
- hidden_out: bfloat16 [4, 4, 64, 4096], P('section', None, 'ep')
The draws below stay inside these ranges and needn't reach their ends.
Inputs may be any that keep to these rules, and one draw needn't show every extreme that they name: `routes`: each row names 8 different experts; within one micro-batch of one layer at most 48 rows name one expert.
All inputs are finite; a program needn't handle non-finite values.
Results may differ from the reference program's by a relative error of at most 0.015.
Values may be sent and summed in bfloat16 or wider, within the bound.
A program may use at most 64 MiB of HBM per device.

```python
import math
import jax
import jax.numpy as jnp
import numpy as np
from jax import lax

D = 4096
FF_E = 1536
MB = 4
LAYERS = 4
EXPERTS = 16
TOP = 8
ROWS = 64
CAP = 48


def level_of(stream_key, extent, cuts, smallest, top_value):
    def one(axis_at, blocks):
        draws = jax.random.uniform(jax.random.fold_in(jax.random.fold_in(stream_key, 6), axis_at), (blocks,), jnp.float32, smallest / len(cuts), top_value / len(cuts))
        return jnp.repeat(jnp.exp(draws), extent[axis_at] // blocks).reshape((-1,) + (1,) * (len(extent) - axis_at - 1))

    level = one(*cuts[0])
    for cut in cuts[1:]:
        level = level * one(*cut)
    return level


def routed_block(rng, own, number, rows, amount, top, most, skew):
    order = jax.random.permutation(rng, amount)
    heavy_load, ordinary = shares(amount, rows * top, most, skew, True), shares(amount, rows * top, most, skew, False)
    places = jnp.arange(amount)

    def named(sizes, offset_by):
        used = int((sizes > 0).sum())
        fixed = max(1, used // 4)
        passed = fixed + (places - fixed + offset_by * (used - fixed)) % max(1, amount - fixed)
        return jnp.zeros((amount,), jnp.int32).at[order[jnp.where(places < fixed, places, passed)]].set(jnp.asarray(sizes, jnp.int32))

    sizes = jnp.where(number % 4 == 0, named(heavy_load, number // 4), named(ordinary, number - number // 4 - 1))
    mixed = jax.random.permutation(jax.random.fold_in(own, 3), amount)
    source_of, receiver = mixed[0:amount // 2 * 2:2], mixed[1:amount // 2 * 2:2]
    margin = jnp.minimum(sizes[source_of] - 1, most - sizes[receiver]) // 2
    margin = jnp.where((source_of == order[0]) | (receiver == order[0]) | (sizes[receiver] == 0), 0, jnp.maximum(margin, 0))
    passed = jax.random.randint(jax.random.fold_in(own, 4), (amount // 2,), 0, 1 << 20) % (margin + 1)
    sizes = sizes.at[source_of].add(-passed).at[receiver].add(passed)
    labels = jnp.searchsorted(jnp.cumsum(sizes), jnp.arange(rows * top), side="right").astype(jnp.int32)
    table = labels.reshape(top, rows).T
    table = table[jax.random.permutation(jax.random.fold_in(own, 1), rows)]
    offset_by = jax.random.randint(jax.random.fold_in(own, 2), (rows, 1), 0, top)
    return jnp.take_along_axis(table, (jnp.arange(top)[None, :] + offset_by) % top, axis=1)


def shares(number_of, total, most, lean, full):
    portions = [(1 << 20) // math.isqrt(standing ** lean) + 1 for standing in range(1, number_of + 1)]
    largest = most if full else min(most, max(-(-total // number_of), total * portions[0] // sum(portions)))
    least = 1 if total - largest >= number_of - 1 else 0
    holding, spare = [largest] + [least] * (number_of - 1), total - largest - least * (number_of - 1)
    while spare > 0:
        movable = [i for i in range(1, number_of) if holding[i] < largest] or [i for i in range(1, number_of) if holding[i] < most]
        whole, remaining = sum([portions[i] for i in movable]), spare
        for i in movable:
            more = min(most - holding[i], max(1, remaining * portions[i] // whole), spare)
            holding[i] = holding[i] + more
            spare = spare - more
    return np.array(holding)


def normal_values(key, extent, spread, bound, pieces=(), held_as=jnp.bfloat16):
    gain = level_of(key, extent, pieces, -0.22, 0.18) if pieces else 1.0
    array = jax.random.normal(key, extent, jnp.float32) * spread * gain
    return jnp.minimum(jnp.maximum(array, -bound), bound).astype(held_as)


def setup_inputs(seed: int = 0) -> dict:
    key_of = jax.random.split(jax.random.key(seed), 8)
    hidden_in = normal_values(key_of[0], (MB, ROWS, D), 0.5, 4.0, ((1, 64),))
    norm_gain = jnp.clip(1.0 + 0.18 * jax.random.normal(key_of[1], (LAYERS, D), jnp.float32), 0.1, 1.9)
    gate_weight = normal_values(key_of[2], (LAYERS, D, EXPERTS * FF_E), D ** -0.5, 0.09375, ((0, 4), (2, 64)))
    up_weight = normal_values(key_of[3], (LAYERS, D, EXPERTS * FF_E), D ** -0.5, 0.09375, ((0, 4), (2, 64)))
    down_weight = normal_values(key_of[4], (LAYERS, EXPERTS * FF_E, D), FF_E ** -0.5, 0.15625, ((0, 4), (1, 64)))
    routes_keys = jax.random.split(jax.random.fold_in(key_of[5], 1), LAYERS * MB * ROWS // ROWS)
    routes_turns = jax.random.permutation(jax.random.fold_in(key_of[5], 3), LAYERS * MB * ROWS // ROWS)
    routes = jax.vmap(lambda own, number: routed_block(jax.random.fold_in(key_of[5], 2), own, number, ROWS, EXPERTS, TOP, CAP, 2))(routes_keys, routes_turns).reshape((LAYERS, MB, ROWS, TOP))
    route_weight = jnp.clip(0.2 + 0.8 * jax.random.uniform(key_of[6], (LAYERS, MB, ROWS, TOP), jnp.float32) ** level_of(key_of[6], (LAYERS, MB, ROWS, TOP), ((0, 4),), -0.2, 0.2), 0.2, 1.0)
    return {"hidden_in": hidden_in, "norm_gain": norm_gain, "gate_weight": gate_weight, "up_weight": up_weight, "down_weight": down_weight, "routes": routes, "route_weight": route_weight}


def reference(hidden_in, norm_gain, gate_weight, up_weight, down_weight, routes, route_weight):
    state = hidden_in.reshape(MB * ROWS, D)
    stacked = []
    for layer in range(LAYERS):
        state_f = state.astype(jnp.float32)
        square = lax.optimization_barrier(jnp.mean(state_f * state_f, axis=-1, keepdims=True))
        normed = (state_f * lax.rsqrt(square + 1e-06) * norm_gain[layer].astype(jnp.float32)).astype(jnp.bfloat16)
        named = routes[layer].reshape(MB * ROWS, TOP)
        weights = route_weight[layer].reshape(MB * ROWS, TOP).astype(jnp.float32)
        weights = weights / lax.optimization_barrier(jnp.sum(weights, axis=-1, keepdims=True))
        w_gate = gate_weight[layer]
        w_up = up_weight[layer]
        w_down = down_weight[layer]

        def expert(carry, index):
            coeff = lax.optimization_barrier(jnp.sum(jnp.where(named == index, weights, jnp.zeros_like(weights)), axis=-1))
            start = (index * FF_E).astype(jnp.int32)
            piece_gate = lax.dynamic_slice_in_dim(w_gate, start, FF_E, 1)
            piece_up = lax.dynamic_slice_in_dim(w_up, start, FF_E, 1)
            piece_down = lax.dynamic_slice_in_dim(w_down, start, FF_E, 0)
            gate = jnp.dot(normed, piece_gate, preferred_element_type=jnp.float32)
            upper = jnp.dot(normed, piece_up, preferred_element_type=jnp.float32)
            act = (jax.nn.silu(gate) * upper).astype(jnp.bfloat16)
            output = jnp.dot(act, piece_down, preferred_element_type=jnp.float32)
            return (carry + coeff[:, None] * output, None)
        moe, unused = lax.scan(expert, jnp.zeros((MB * ROWS, D), jnp.float32), jnp.arange(EXPERTS, dtype=jnp.int32))
        state = (state_f + moe).astype(jnp.bfloat16)
        stacked.append(state.reshape(MB, ROWS, D))
    return jnp.stack(stacked)
```

```python
import functools

import jax
import jax.numpy as jnp
from jax import lax
from jax.experimental import pallas as pl
from jax.experimental.pallas import tpu as pltpu
from jax.sharding import PartitionSpec as P

MESH = pl.DeviceIdType.MESH
BF = jnp.bfloat16
F32 = jnp.float32

D = 4096
FF = 384
MB = 4
SECTIONS = 4
YS, ZS = 4, 8
ROWS = 64
RB = 16
FB = 256
HALF = D // 2
CH = 512
FAR_FIRST = (4, 3, 5, 2, 6, 1, 7)
NEAR_FIRST = (0, 1, 7, 2, 6, 3, 5, 4)
CHUNK_ORDER = (2, 1, 3, 0)

SCHEDULE = (("A", 0), ("E", 2), ("C", 1), ("D", 1), ("F", 2), ("B", 0))
SLOTS = MB + 2


def mo(value, by):
    return pl.multiple_of(value, by)


def wait(ref, sem):
    pltpu.make_async_copy(ref, ref, sem).wait()


def kernel(
    hin, gain, wg_hbm, wu_hbm, wd_hbm, routes, rweight, out,
    wg, wu, wd, xg, hin_f, tin, coeff, act_s, pc, rsc, part, py, rsy, pz, rsz,
    res, oblk, out_t, orow,
    w_sem, tin_r, tin_s, agz_r, agy_r, agc_r, rsc_r, rsy_r, rsz_r, res_r, ob_r, or_r, or_s,
    s_a, s_res, s_ob, s_b, s_c, s_d, s_e, s_f,
):
    s = lax.axis_index("section")
    ep = lax.axis_index("ep")
    y = ep // 16
    q = ep % 16
    z = q // 2
    c = q % 2
    b = c * ZS + z
    plane = y * 16
    partner = (s, plane + z * 2 + (1 - c))
    row0 = mo(y * RB, RB)
    col0 = mo(b * FB, FB)
    half0 = mo(c * HALF, HALF)
    half1 = mo((1 - c) * HALF, HALF)

    def at(sec, yy, zz, cc):
        return (sec, yy * 16 + zz * 2 + cc)

    def send(src, dst, ss, rs, device):
        pltpu.make_async_remote_copy(
            src_ref=src, dst_ref=dst, send_sem=ss, recv_sem=rs, device_id=device, device_id_type=MESH
        ).start()

    weights = [
        pltpu.make_async_copy(wg_hbm.at[0], wg, w_sem.at[0]),
        pltpu.make_async_copy(wu_hbm.at[0], wu, w_sem.at[1]),
        pltpu.make_async_copy(wd_hbm.at[0], wd, w_sem.at[2]),
    ]
    for copy in weights:
        copy.start()

    barrier = pltpu.get_barrier_semaphore()

    def greet(device):
        pl.semaphore_signal(barrier, inc=1, device_id=device, device_id_type=MESH)

    def greet_plane(j, _):
        greet((s, plane + (q + j) % 16))
        return 0

    lax.fori_loop(1, 16, greet_plane, 0)
    for dy in (1, 2, 3):
        greet(at(s, (y + dy) % YS, z, c))

    def greet_next(j, _):
        greet(at(s + 1, y, j, c))
        return 0

    def greet_last(j, _):
        greet(at(s - 1, y, j, c))
        return 0

    @pl.when(s < SECTIONS - 1)
    def _():
        lax.fori_loop(0, ZS, greet_next, 0)

    @pl.when(s > 0)
    def _():
        lax.fori_loop(0, ZS, greet_last, 0)

    expert = ep // 4
    rw = rweight[0].reshape(MB * ROWS, 8)
    named = routes[0].reshape(MB * ROWS, 8) == expert
    hit = jnp.sum(jnp.where(named, rw, 0.0), axis=-1, keepdims=True)
    total = jnp.sum(rw, axis=-1, keepdims=True)
    coeff[...] = jnp.broadcast_to(hit / total, (MB * ROWS, 128))
    hin_f[...] = jnp.zeros_like(hin_f)
    hin_f[0:MB, :] = hin[:, 0, :].astype(F32)
    out_t[...] = jnp.zeros_like(out_t)

    inner = jnp.logical_and(s > 0, s < SECTIONS - 1)
    pl.semaphore_wait(barrier, jnp.where(inner, 18 + 2 * ZS, 18 + ZS))

    @pl.when(s == 0)
    def _():
        def spread(j, _):
            qq = (q + j) % 16
            bb = (qq % 2) * ZS + qq // 2
            send(hin_f.at[:, pl.ds(mo(bb * FB, FB), FB)], tin.at[q], tin_s, tin_r, (s, plane + qq))
            return 0

        lax.fori_loop(1, 16, spread, 0)
        tin[q] = hin_f[:, pl.ds(col0, FB)]
        wait(tin.at[pl.ds(0, 15)], tin_r)

    def block(m, yy, bb):
        return xg.at[m, pl.ds(mo(yy * RB, RB), RB), pl.ds(mo(bb * FB, FB), FB)]

    def summed(where, m, start):
        total = start
        for k in range(ZS):
            total = total + rsz[where, m, k].astype(F32)
        return total

    def phase_a(m):
        @pl.when(s == 0)
        def _():
            xg[m, pl.ds(row0, RB), pl.ds(col0, FB)] = tin[:, m, :].astype(BF)

        @pl.when(s > 0)
        def _():
            wait(res.at[m], res_r.at[m])
            wait(rsz.at[0, m], rsz_r.at[0, m])
            xg[m, pl.ds(row0, RB), pl.ds(col0, FB)] = summed(0, m, res[m].astype(F32)).astype(BF)

        mine = block(m, y, b)
        for off in FAR_FIRST:
            send(mine, mine, s_a.at[m], agz_r.at[m, z], at(s, y, (z + off) % ZS, c))

        @pl.when(s < SECTIONS - 1)
        def _():
            send(mine, res.at[m], s_res.at[m], res_r.at[m], at(s + 1, y, z, c))

        @pl.when(s > 0)
        def _():
            send(mine, oblk.at[m], s_ob.at[m], ob_r.at[m], at(s - 1, y, z, c))

    def phase_b(m):
        for off in NEAR_FIRST:
            zz = (z + off) % ZS
            piece = block(m, y, c * ZS + zz)
            if off:
                wait(piece, agz_r.at[m, zz])
            for dy in (2, 1, 3):
                send(piece, piece, s_b.at[m], agy_r.at[m, dy - 1], at(s, (y + dy) % YS, z, c))
        rows = xg.at[m, pl.ds(row0, RB), pl.ds(half0, HALF)]
        send(rows, rows, s_c.at[m], agc_r.at[m], partner)

    def phase_c(m):
        for dy in (1, 3, 2):
            yy = (y + YS - dy) % YS
            rows = xg.at[m, pl.ds(mo(yy * RB, RB), RB), pl.ds(half0, HALF)]
            wait(rows, agy_r.at[m, dy - 1])
            send(rows, rows, s_c.at[m], agc_r.at[m], partner)

    def phase_d(m):
        def up_to(start, carry):
            g, u, ss = carry
            for k in range(HALF // CH):
                cols = pl.ds(mo(start + k * CH, CH), CH)
                h = xg[m, :, cols].astype(F32)
                sq = h * h
                for j in range(CH // 128):
                    ss = ss + sq[:, j * 128 : (j + 1) * 128]
                hg = (h * gain[:, cols]).astype(BF)
                g = g + jnp.dot(hg, wg[cols, :], preferred_element_type=F32)
                u = u + jnp.dot(hg, wu[cols, :], preferred_element_type=F32)
            return g, u, ss

        carry = (jnp.zeros((ROWS, FF), F32), jnp.zeros((ROWS, FF), F32), jnp.zeros((ROWS, 128), F32))
        carry = up_to(half0, carry)
        wait(xg.at[m, :, pl.ds(half1, HALF)], agc_r.at[m])
        g, u, ss = up_to(half1, carry)
        scale = lax.rsqrt(jnp.sum(ss, axis=-1, keepdims=True) * (1.0 / D) + 1e-06)
        g = g * scale
        co = coeff[pl.ds(mo(m * ROWS, ROWS), ROWS), 0:1]
        act_s[...] = (jax.nn.silu(g) * (u * scale) * co).astype(BF)
        for t, off in enumerate(CHUNK_ORDER):
            piece = (z // 2 + off) % 4
            src = mo((1 - c) * HALF + piece * CH, CH)
            cols = pl.ds(mo(piece * CH, CH), CH)
            pc[m, :, cols] = jnp.dot(act_s[...], wd[:, pl.ds(src, CH)], preferred_element_type=F32).astype(BF)
            send(pc.at[m, :, cols], rsc.at[m, :, cols], s_d.at[m], rsc_r.at[m, t], partner)
        for off in CHUNK_ORDER:
            piece = (z // 2 + off) % 4
            src = mo(c * HALF + piece * CH, CH)
            cols = pl.ds(mo(piece * CH, CH), CH)
            part[m, :, cols] = jnp.dot(act_s[...], wd[:, pl.ds(src, CH)], preferred_element_type=F32)

    def phase_e(m):
        for t, off in enumerate(CHUNK_ORDER):
            cols = pl.ds(mo(((z // 2 + off) % 4) * CH, CH), CH)
            wait(rsc.at[m, :, cols], rsc_r.at[m, t])
            py[m, :, cols] = (part[m, :, cols] + rsc[m, :, cols].astype(F32)).astype(BF)
            for dy in (2, 1, 3):
                yy = (y + dy) % YS
                send(
                    py.at[m, pl.ds(mo(yy * RB, RB), RB), cols],
                    rsy.at[m, pl.ds((dy - 1) * RB, RB), cols],
                    s_e.at[m], rsy_r.at[m, t], at(s, yy, z, c),
                )

    def phase_f(m):
        last = s == SECTIONS - 1
        to = jnp.where(last, s, s + 1)
        where = jnp.where(last, 1, 0)
        for t, off in enumerate(CHUNK_ORDER):
            piece = (z // 2 + off) % 4
            cols = pl.ds(mo(piece * CH, CH), CH)
            wait(rsy.at[m, :, cols], rsy_r.at[m, t])
            total = py[m, pl.ds(row0, RB), cols].astype(F32)
            for k in range(YS - 1):
                total = total + rsy[m, k * RB : (k + 1) * RB, cols].astype(F32)
            pz[m, :, cols] = total.astype(BF)
            for e in range(2):
                zz = piece * 2 + e
                src = pz.at[m, :, pl.ds(mo(zz * FB, FB), FB)]
                dst = rsz.at[where, m, z]
                here = jnp.logical_and(last, zz == z)

                @pl.when(here)
                def _():
                    pltpu.make_async_copy(src, dst, rsz_r.at[where, m]).start()

                @pl.when(jnp.logical_not(here))
                def _():
                    send(src, dst, s_f.at[m], rsz_r.at[where, m], at(to, y, zz, c))

    phases = {"A": phase_a, "B": phase_b, "C": phase_c, "D": phase_d, "E": phase_e, "F": phase_f}

    def slot(n, _):
        for name, lag in SCHEDULE:
            m = n - lag

            if name == "D":
                @pl.when(m == 0)
                def _():
                    for copy in weights:
                        copy.wait()

            @pl.when(jnp.logical_and(m >= 0, m < MB))
            def _():
                phases[name](m)

        return 0

    lax.fori_loop(0, SLOTS, slot, 0)

    for m in range(MB):
        @pl.when(s == SECTIONS - 1)
        def _():
            wait(rsz.at[1, m], rsz_r.at[1, m])
            start = xg[m, pl.ds(row0, RB), pl.ds(col0, FB)].astype(F32)
            oblk[m] = summed(1, m, start).astype(BF)

        @pl.when(s < SECTIONS - 1)
        def _():
            wait(oblk.at[m], ob_r.at[m])

        out_t[:, m, :] = oblk[m].astype(F32)

    def collect(j, _):
        qq = (q + j) % 16
        send(out_t.at[qq], orow.at[b], or_s, or_r, (s, plane + qq))
        return 0

    lax.fori_loop(1, 16, collect, 0)
    orow[b] = out_t[q]
    wait(orow.at[pl.ds(0, 15)], or_r)
    for k in range(2 * ZS):
        out[0, :, 0, k * FB : (k + 1) * FB] = orow[k, 0:MB, :].astype(BF)

    @pl.when(s == 0)
    def _():
        wait(tin.at[pl.ds(0, 15)], tin_s)

    wait(orow.at[pl.ds(0, 15)], or_s)
    for m in range(MB):
        wait(xg.at[m, pl.ds(0, RB), pl.ds(0, 7 * FB)], s_a.at[m])
        wait(xg.at[m, pl.ds(0, 3 * RB), pl.ds(0, HALF)], s_b.at[m])
        wait(xg.at[m, :, pl.ds(0, HALF)], s_c.at[m])
        wait(pc.at[m], s_d.at[m])
        wait(rsy.at[m], s_e.at[m])

        @pl.when(s < SECTIONS - 1)
        def _():
            wait(rsz.at[0, m], s_f.at[m])
            wait(res.at[m], s_res.at[m])

        @pl.when(s == SECTIONS - 1)
        def _():
            wait(rsz.at[0, m, pl.ds(0, ZS - 1)], s_f.at[m])

        @pl.when(s > 0)
        def _():
            wait(oblk.at[m], s_ob.at[m])


def local(hidden_in, norm_gain, gate_weight, up_weight, down_weight, routes, route_weight):
    vmem = pl.BlockSpec(memory_space=pltpu.VMEM)
    hbm = pl.BlockSpec(memory_space=pl.ANY)
    dma = pltpu.SemaphoreType.DMA
    return pl.pallas_call(
        kernel,
        name="moe_layers",
        out_shape=jax.ShapeDtypeStruct((1, MB, 1, D), BF),
        in_specs=[vmem, vmem, hbm, hbm, hbm, vmem, vmem],
        out_specs=vmem,
        scratch_shapes=[
            pltpu.VMEM((D, FF), BF),
            pltpu.VMEM((D, FF), BF),
            pltpu.VMEM((FF, D), BF),
            pltpu.VMEM((MB, ROWS, D), BF),
            pltpu.VMEM((8, D), F32),
            pltpu.VMEM((16, 8, FB), F32),
            pltpu.VMEM((MB * ROWS, 128), F32),
            pltpu.VMEM((ROWS, FF), BF),
            pltpu.VMEM((MB, ROWS, HALF), BF),
            pltpu.VMEM((MB, ROWS, HALF), BF),
            pltpu.VMEM((MB, ROWS, HALF), F32),
            pltpu.VMEM((MB, ROWS, HALF), BF),
            pltpu.VMEM((MB, 3 * RB, HALF), BF),
            pltpu.VMEM((MB, RB, HALF), BF),
            pltpu.VMEM((2, MB, ZS, RB, FB), BF),
            pltpu.VMEM((MB, RB, FB), BF),
            pltpu.VMEM((MB, RB, FB), BF),
            pltpu.VMEM((16, 8, FB), F32),
            pltpu.VMEM((16, 8, FB), F32),
            dma((3,)),
            dma, dma,
            dma((MB, ZS)),
            dma((MB, 3)),
            dma((MB,)),
            dma((MB, 4)),
            dma((MB, 4)),
            dma((2, MB)),
            dma((MB,)),
            dma((MB,)),
            dma, dma,
            dma((MB,)), dma((MB,)), dma((MB,)), dma((MB,)), dma((MB,)), dma((MB,)), dma((MB,)), dma((MB,)),
        ],
        compiler_params=pltpu.CompilerParams(
            collective_id=0, has_side_effects=True, vmem_limit_bytes=48 << 20
        ),
        cost_estimate=pl.CostEstimate(
            flops=6 * MB * ROWS * D * FF, bytes_accessed=6 * D * FF, transcendentals=MB * ROWS * FF
        ),
    )(hidden_in, norm_gain, gate_weight, up_weight, down_weight, routes, route_weight)


def solution(mesh):
    return jax.shard_map(
        local,
        mesh=mesh,
        in_specs=(
            P(None, "ep", None),
            P("section", None),
            P("section", None, "ep"),
            P("section", None, "ep"),
            P("section", "ep", None),
            P("section", None, None, None),
            P("section", None, None, None),
        ),
        out_specs=P("section", None, "ep", None),
        check_vma=False,
    )
```

```python
import functools

import jax
import jax.numpy as jnp
from jax import lax
from jax.experimental import pallas as pl
from jax.experimental.pallas import tpu as pltpu
from jax.sharding import PartitionSpec as P

MESH = pl.DeviceIdType.MESH
BF = jnp.bfloat16
F32 = jnp.float32

D = 4096
FF = 384
MB = 4
SECTIONS = 4
YS, ZS = 4, 8
ROWS = 64
RB = 16
FB = 256
HALF = D // 2
CH = 512
PIECES = HALF // CH
FAR_FIRST = (4, 3, 5, 2, 6, 1, 7)
GATHER_ORDER = (0, 1, 3, 2)
SUM_ORDER = (2, 1, 3, 0)

SCHEDULE = (("A", 0), ("D", 2), ("G", 2), ("F", 3), ("E", 2), ("C", 1), ("B", 0))
SLOTS = MB + 3


def mo(value, by):
    return pl.multiple_of(value, by)


def wait(ref, sem):
    pltpu.make_async_copy(ref, ref, sem).wait()


def kernel(
    hin_hbm, gain_hbm, wg_hbm, wu_hbm, wd_hbm, routes_hbm, rweight_hbm, out,
    hin, gain, routes, rweight, wg, wu, wd, xg, hin_f, tin, coeff, act_s, pc, rsc, part, py, rsy, pz, rsz,
    res, oblk, out_t, orow, hin_0, tin_0, pzf, orow_l,
    w_sem, tin_r, tin_s, tin0_r, tin0_s, orl_r, agz_r, agy_r, agc_r, rsc_r, rsy_r, rsz_r, res_r, ob_r, or_r, or_s,
    s_a, s_res, s_ob, s_b, s_c, s_d, s_e, s_f,
):
    s = lax.axis_index("section")
    ep = lax.axis_index("ep")
    y = ep // 16
    q = ep % 16
    z = q // 2
    c = q % 2
    b = c * ZS + z
    plane = y * 16
    partner = (s, plane + z * 2 + (1 - c))
    row0 = mo(y * RB, RB)
    col0 = mo(b * FB, FB)
    half0 = mo(c * HALF, HALF)
    half1 = mo((1 - c) * HALF, HALF)

    def at(sec, yy, zz, cc):
        return (sec, yy * 16 + zz * 2 + cc)

    def send(src, dst, ss, rs, device):
        pltpu.make_async_remote_copy(
            src_ref=src, dst_ref=dst, send_sem=ss, recv_sem=rs, device_id=device, device_id_type=MESH
        ).start()

    small = [
        pltpu.make_async_copy(hin_hbm, hin, w_sem.at[3]),
        pltpu.make_async_copy(gain_hbm, gain, w_sem.at[4]),
        pltpu.make_async_copy(routes_hbm, routes, w_sem.at[5]),
        pltpu.make_async_copy(rweight_hbm, rweight, w_sem.at[6]),
    ]
    for copy in small:
        copy.start()
    weights = [
        pltpu.make_async_copy(wg_hbm.at[0], wg, w_sem.at[0]),
        pltpu.make_async_copy(wu_hbm.at[0], wu, w_sem.at[1]),
        pltpu.make_async_copy(wd_hbm.at[0], wd, w_sem.at[2]),
    ]
    for copy in weights:
        copy.start()

    barrier = pltpu.get_barrier_semaphore()

    def greet(device):
        pl.semaphore_signal(barrier, inc=1, device_id=device, device_id_type=MESH)

    def greet_plane(j, _):
        greet((s, plane + (q + j) % 16))
        return 0

    lax.fori_loop(1, 16, greet_plane, 0)
    for dy in (1, 2, 3):
        greet(at(s, (y + dy) % YS, z, c))

    def greet_next(j, _):
        greet(at(s + 1, y, j, c))
        return 0

    def greet_last(j, _):
        greet(at(s - 1, y, j, c))
        return 0

    @pl.when(s < SECTIONS - 1)
    def _():
        lax.fori_loop(0, ZS, greet_next, 0)

    @pl.when(s > 0)
    def _():
        lax.fori_loop(0, ZS, greet_last, 0)

    for copy in small:
        copy.wait()
    expert = ep // 4
    for m in range(MB):
        rw = rweight[0, m]
        hit = jnp.sum(jnp.where(routes[0, m] == expert, rw, 0.0), axis=0, keepdims=True)
        share = hit / jnp.sum(rw, axis=0, keepdims=True)
        coeff[m] = jnp.swapaxes(jnp.broadcast_to(share, (128, ROWS)), 0, 1)
    hin_f[...] = jnp.zeros_like(hin_f)
    hin_f[0:MB, :] = hin[...].astype(F32)
    for k in range(2 * ZS):
        hin_0[k // ZS, k % ZS : k % ZS + 1, :] = hin_f[0:1, k * FB : (k + 1) * FB]
    out_t[...] = jnp.zeros_like(out_t)

    inner = jnp.logical_and(s > 0, s < SECTIONS - 1)
    pl.semaphore_wait(barrier, jnp.where(inner, 18 + 2 * ZS, 18 + ZS))

    def ring(k):
        return (q + 8 + (1 - 2 * (k % 2)) * ((k + 1) // 2)) % 16

    @pl.when(s == 0)
    def _():
        def spread_0(k, _):
            qq = ring(k)
            send(hin_0.at[qq % 2], tin_0.at[q], tin0_s, tin0_r, (s, plane + qq))
            return 0

        lax.fori_loop(0, 15, spread_0, 0)
        pltpu.make_async_copy(hin_0.at[c], tin_0.at[q], tin0_r).start()

    def block(m, yy, bb):
        return xg.at[m, pl.ds(mo(yy * RB, RB), RB), pl.ds(mo(bb * FB, FB), FB)]

    def phase_a(m):
        first = jnp.logical_and(s == 0, m == 0)

        @pl.when(first)
        def _():
            wait(tin_0, tin0_r)
            for k in range(ZS):
                xg[m, pl.ds(row0, RB), pl.ds(mo(half0 + k * FB, FB), FB)] = tin_0[:, k, :].astype(BF)

            def spread(k, _):
                qq = ring(k)
                bb = (qq % 2) * ZS + qq // 2
                send(hin_f.at[:, pl.ds(mo(bb * FB, FB), FB)], tin.at[q], tin_s, tin_r, (s, plane + qq))
                return 0

            lax.fori_loop(0, 15, spread, 0)
            tin[q] = hin_f[:, pl.ds(col0, FB)]

        @pl.when(jnp.logical_and(s == 0, m == 1))
        def _():
            wait(tin.at[pl.ds(0, 15)], tin_r)

        @pl.when(jnp.logical_and(s == 0, m > 0))
        def _():
            xg[m, pl.ds(row0, RB), pl.ds(col0, FB)] = tin[:, m, :].astype(BF)

        @pl.when(s > 0)
        def _():
            wait(res.at[m], res_r.at[m])
            wait(rsz.at[m], rsz_r.at[m])
            total = res[m].astype(F32)
            for k in range(ZS):
                total = total + rsz[m, k].astype(F32)
            xg[m, pl.ds(row0, RB), pl.ds(col0, FB)] = total.astype(BF)

        mine = block(m, y, b)

        @pl.when(jnp.logical_not(first))
        def _():
            for off in FAR_FIRST:
                send(mine, mine, s_a.at[m], agz_r.at[m, z], at(s, y, (z + off) % ZS, c))

        @pl.when(s < SECTIONS - 1)
        def _():
            send(mine, res.at[m], s_res.at[m], res_r.at[m], at(s + 1, y, z, c))

        @pl.when(s > 0)
        def _():
            send(mine, oblk.at[m], s_ob.at[m], ob_r.at[m], at(s - 1, y, z, c))

    def gather_cols(t, start):
        return pl.ds(mo(start + ((z // 2 + GATHER_ORDER[t]) % PIECES) * CH, CH), CH)

    def phase_b(m):
        for t in range(PIECES):
            @pl.when(jnp.logical_or(s > 0, m > 0))
            def _():
                pair = ((z // 2 + GATHER_ORDER[t]) % PIECES) * 2
                for zz in (pair + 1 - z % 2,) if t == 0 else (pair, pair + 1):
                    wait(block(m, y, c * ZS + zz), agz_r.at[m, zz])

            piece = xg.at[m, pl.ds(row0, RB), gather_cols(t, half0)]
            for dy in (2, 1, 3):
                send(piece, piece, s_b.at[m], agy_r.at[m, t], at(s, (y + dy) % YS, z, c))

    def to_partner(m, t):
        cols = gather_cols(t, half0)
        wait(xg.at[m, pl.ds(0, 3 * RB), cols], agy_r.at[m, t])
        piece = xg.at[m, :, cols]
        send(piece, piece, s_c.at[m], agc_r.at[m, t], partner)

    def products(m, cols, carry):
        g, u, ss = carry
        h = xg[m, :, cols].astype(F32)
        sq = h * h
        for j in range(CH // 128):
            ss = ss + sq[:, j * 128 : (j + 1) * 128]
        hg = (h * gain[:, cols]).astype(BF)
        g = g + jnp.dot(hg, wg[cols, :], preferred_element_type=F32)
        u = u + jnp.dot(hg, wu[cols, :], preferred_element_type=F32)
        return g, u, ss

    def from_partner(m, t, carry):
        cols = gather_cols(t, half1)
        wait(xg.at[m, :, cols], agc_r.at[m, t])
        return products(m, cols, carry)

    def start_sums():
        return jnp.zeros((ROWS, FF), F32), jnp.zeros((ROWS, FF), F32), jnp.zeros((ROWS, 128), F32)

    def activate(m, carry):
        g, u, ss = carry
        scale = lax.rsqrt(jnp.sum(ss, axis=-1, keepdims=True) * (1.0 / D) + 1e-06)
        g = g * scale
        act_s[m] = (jax.nn.silu(g) * (u * scale) * coeff[m, :, 0:1]).astype(BF)

    def phase_c(m):
        for t in range(PIECES):
            to_partner(m, t)

    def phase_d(m):
        carry = start_sums()
        for t in range(PIECES):
            carry = products(m, gather_cols(t, half0), carry)
        for t in range(PIECES):
            carry = from_partner(m, t, carry)
        activate(m, carry)

    def phase_k(m):
        carry = start_sums()
        for t in range(PIECES):
            to_partner(m, t)
            carry = products(m, gather_cols(t, half0), carry)
            if t:
                carry = from_partner(m, t - 1, carry)
        activate(m, from_partner(m, PIECES - 1, carry))

    def phase_g(m):
        for t, off in enumerate(SUM_ORDER):
            piece = (z // 2 + off) % PIECES
            src = mo((1 - c) * HALF + piece * CH, CH)
            cols = pl.ds(mo(piece * CH, CH), CH)
            pc[m, :, cols] = jnp.dot(act_s[m], wd[:, pl.ds(src, CH)], preferred_element_type=F32).astype(BF)
            send(pc.at[m, :, cols], rsc.at[m, :, cols], s_d.at[m], rsc_r.at[m, t], partner)
        for off in SUM_ORDER:
            piece = (z // 2 + off) % PIECES
            src = mo(c * HALF + piece * CH, CH)
            cols = pl.ds(mo(piece * CH, CH), CH)
            part[m, :, cols] = jnp.dot(act_s[m], wd[:, pl.ds(src, CH)], preferred_element_type=F32)

    def phase_e(m):
        for t, off in enumerate(SUM_ORDER):
            cols = pl.ds(mo(((z // 2 + off) % 4) * CH, CH), CH)
            wait(rsc.at[m, :, cols], rsc_r.at[m, t])
            py[m, :, cols] = (part[m, :, cols] + rsc[m, :, cols].astype(F32)).astype(BF)
            for dy in (2, 1, 3):
                yy = (y + dy) % YS
                send(
                    py.at[m, pl.ds(mo(yy * RB, RB), RB), cols],
                    rsy.at[m, pl.ds((dy - 1) * RB, RB), cols],
                    s_e.at[m], rsy_r.at[m, t], at(s, yy, z, c),
                )

    def phase_f(m):
        last = s == SECTIONS - 1
        for t, off in enumerate(SUM_ORDER):
            piece = (z // 2 + off) % PIECES
            cols = pl.ds(mo(piece * CH, CH), CH)
            wait(rsy.at[m, :, cols], rsy_r.at[m, t])
            total = py[m, pl.ds(row0, RB), cols].astype(F32)
            for k in range(YS - 1):
                total = total + rsy[m, k * RB : (k + 1) * RB, cols].astype(F32)

            @pl.when(s < SECTIONS - 1)
            def _():
                pz[m, :, cols] = total.astype(BF)
                for e in range(2):
                    zz = piece * 2 + e
                    src = pz.at[m, :, pl.ds(mo(zz * FB, FB), FB)]
                    send(src, rsz.at[m, z], s_f.at[m], rsz_r.at[m], at(s + 1, y, zz, c))

            @pl.when(last)
            def _():
                for e in range(2):
                    pzf[m, :, piece * 2 + e, :] = total[:, e * FB : (e + 1) * FB]

        @pl.when(last)
        def _():
            pzf[m, :, z, :] = pzf[m, :, z, :] + xg[m, pl.ds(row0, RB), pl.ds(col0, FB)].astype(F32)

            def give(k, _):
                qq = ring(k)
                send(pzf.at[m, qq], orow_l.at[m, q], s_f.at[m], orl_r.at[m], (s, plane + qq))
                return 0

            lax.fori_loop(0, 15, give, 0)
            pltpu.make_async_copy(pzf.at[m, q], orow_l.at[m, q], orl_r.at[m]).start()

    phases = {"A": phase_a, "B": phase_b, "C": phase_c, "D": phase_d, "K": phase_k, "G": phase_g, "E": phase_e, "F": phase_f}

    def slot(n, _):
        for name, lag in SCHEDULE:
            m = n - lag

            if name in "DK":
                @pl.when(m == 0)
                def _():
                    for copy in weights:
                        copy.wait()

            @pl.when(jnp.logical_and(m >= 0, m < MB))
            def _():
                phases[name](m)

        return 0

    lax.fori_loop(0, SLOTS, slot, 0)

    @pl.when(s < SECTIONS - 1)
    def _():
        for m in range(MB):
            wait(oblk.at[m], ob_r.at[m])
            out_t[:, m, :] = oblk[m].astype(F32)

        def collect(k, _):
            qq = ring(k)
            send(out_t.at[qq], orow.at[b], or_s, or_r, (s, plane + qq))
            return 0

        lax.fori_loop(0, 15, collect, 0)
        orow[b] = out_t[q]
        wait(orow.at[pl.ds(0, 15)], or_r)

    @pl.when(s == SECTIONS - 1)
    def _():
        for m in range(MB):
            wait(orow_l.at[m], orl_r.at[m])
            for cc in range(2):
                total = orow_l[m, cc]
                for k in range(1, ZS):
                    total = total + orow_l[m, 2 * k + cc]
                orow[cc * ZS : (cc + 1) * ZS, m, :] = total

    for k in range(2 * ZS):
        out[:, k * FB : (k + 1) * FB] = orow[k, 0:MB, :].astype(BF)

    @pl.when(s == 0)
    def _():
        wait(tin_0.at[pl.ds(0, 15)], tin0_s)
        wait(tin.at[pl.ds(0, 15)], tin_s)

    @pl.when(s < SECTIONS - 1)
    def _():
        wait(orow.at[pl.ds(0, 15)], or_s)

    for m in range(MB):
        def gathered(m=m):
            wait(xg.at[m, pl.ds(0, RB), pl.ds(0, 7 * FB)], s_a.at[m])

        if m:
            gathered()
        else:
            pl.when(s > 0)(gathered)
        wait(xg.at[m, pl.ds(0, 3 * RB), pl.ds(0, HALF)], s_b.at[m])
        wait(xg.at[m, :, pl.ds(0, HALF)], s_c.at[m])
        wait(pc.at[m], s_d.at[m])
        wait(rsy.at[m], s_e.at[m])

        @pl.when(s < SECTIONS - 1)
        def _():
            wait(rsz.at[m], s_f.at[m])
            wait(res.at[m], s_res.at[m])

        @pl.when(s == SECTIONS - 1)
        def _():
            wait(orow_l.at[m, pl.ds(0, 15)], s_f.at[m])

        @pl.when(s > 0)
        def _():
            wait(oblk.at[m], s_ob.at[m])


def local(hidden_in, norm_gain, gate_weight, up_weight, down_weight, routes, route_weight):
    vmem = pl.BlockSpec(memory_space=pltpu.VMEM)
    hbm = pl.BlockSpec(memory_space=pl.ANY)
    dma = pltpu.SemaphoreType.DMA
    rows = pl.pallas_call(
        kernel,
        name="moe_layers",
        out_shape=jax.ShapeDtypeStruct((MB, D), BF),
        in_specs=[hbm] * 7,
        out_specs=vmem,
        scratch_shapes=[
            pltpu.VMEM((MB, D), BF),
            pltpu.VMEM((1, D), F32),
            pltpu.VMEM((1, MB, 8, ROWS), jnp.int32),
            pltpu.VMEM((1, MB, 8, ROWS), F32),
            pltpu.VMEM((D, FF), BF),
            pltpu.VMEM((D, FF), BF),
            pltpu.VMEM((FF, D), BF),
            pltpu.VMEM((MB, ROWS, D), BF),
            pltpu.VMEM((8, D), F32),
            pltpu.VMEM((16, 8, FB), F32),
            pltpu.VMEM((MB, ROWS, 128), F32),
            pltpu.VMEM((MB, ROWS, FF), BF),
            pltpu.VMEM((MB, ROWS, HALF), BF),
            pltpu.VMEM((MB, ROWS, HALF), BF),
            pltpu.VMEM((MB, ROWS, HALF), F32),
            pltpu.VMEM((MB, ROWS, HALF), BF),
            pltpu.VMEM((MB, 3 * RB, HALF), BF),
            pltpu.VMEM((MB, RB, HALF), BF),
            pltpu.VMEM((MB, ZS, RB, FB), BF),
            pltpu.VMEM((MB, RB, FB), BF),
            pltpu.VMEM((MB, RB, FB), BF),
            pltpu.VMEM((16, 8, FB), F32),
            pltpu.VMEM((16, 8, FB), F32),
            pltpu.VMEM((2, ZS, FB), F32),
            pltpu.VMEM((16, ZS, FB), F32),
            pltpu.VMEM((MB, 16, ZS, FB), F32),
            pltpu.VMEM((MB, 16, ZS, FB), F32),
            dma((7,)),
            dma, dma,
            dma, dma,
            dma((MB,)),
            dma((MB, ZS)),
            dma((MB, PIECES)),
            dma((MB, PIECES)),
            dma((MB, 4)),
            dma((MB, 4)),
            dma((MB,)),
            dma((MB,)),
            dma((MB,)),
            dma, dma,
            dma((MB,)), dma((MB,)), dma((MB,)), dma((MB,)), dma((MB,)), dma((MB,)), dma((MB,)), dma((MB,)),
        ],
        compiler_params=pltpu.CompilerParams(
            collective_id=0, has_side_effects=True, vmem_limit_bytes=60 << 20
        ),
        cost_estimate=pl.CostEstimate(
            flops=6 * MB * ROWS * D * FF, bytes_accessed=6 * D * FF, transcendentals=MB * ROWS * FF
        ),
    )(
        hidden_in.reshape(MB, D),
        norm_gain,
        gate_weight,
        up_weight,
        down_weight,
        jnp.swapaxes(routes, 2, 3),
        jnp.swapaxes(route_weight, 2, 3),
    )
    return rows[None, :, None, :]


def solution(mesh):
    return jax.shard_map(
        local,
        mesh=mesh,
        in_specs=(
            P(None, "ep", None),
            P("section", None),
            P("section", None, "ep"),
            P("section", None, "ep"),
            P("section", "ep", None),
            P("section", None, None, None),
            P("section", None, None, None),
        ),
        out_specs=P("section", None, "ep", None),
        check_vma=False,
    )
```

```python
import functools

import jax
import jax.numpy as jnp
from jax import lax
from jax.experimental import pallas as pl
from jax.experimental.pallas import tpu as pltpu
from jax.sharding import PartitionSpec as P

MESH = pl.DeviceIdType.MESH
BF = jnp.bfloat16
F32 = jnp.float32

D = 4096
FF = 384
MB = 4
SECTIONS = 4
YS, ZS = 4, 8
ROWS = 64
RB = 16
FB = 256
HALF = D // 2
CH = 512
PIECES = HALF // CH
GROUP = CH // FB
FAR_FIRST = (4, 3, 5, 2, 6, 1, 7)
GATHER_ORDER = (0, 1, 3, 2)
SUM_ORDER = (2, 1, 3, 0)

SCHEDULE = (("A", 0), ("D", 2), ("G", 2), ("F", 3), ("E", 2), ("C", 1), ("B", 0))
SLOTS = MB + 3


def mo(value, by):
    return pl.multiple_of(value, by)


def wait(ref, sem):
    pltpu.make_async_copy(ref, ref, sem).wait()


def kernel(
    hin_hbm, gain_hbm, wg_hbm, wu_hbm, wd_hbm, routes_hbm, rweight_hbm, out,
    hin, gain, routes, rweight, wg, wu, wd, xg, hin_f, tin, coeff, act_s, pc, rsc, part, py, rsy, pz, rsz,
    res, oblk, out_t, orow, hin_0, tin_0, pzf, orow_l,
    w_sem, tin_r, tin_s, tin0_r, tin0_s, orl_r, agz_r, agy_r, agc_r, rsc_r, rsy_r, rsz_r, res_r, ob_r, or_r, or_s,
    s_a, s_res, s_ob, s_b, s_c, s_d, s_e, s_f,
):
    s = lax.axis_index("section")
    ep = lax.axis_index("ep")
    y = ep // 16
    q = ep % 16
    z = q // 2
    c = q % 2
    b = c * ZS + z
    plane = y * 16
    partner = (s, plane + z * 2 + (1 - c))
    row0 = mo(y * RB, RB)
    col0 = mo(b * FB, FB)
    half0 = mo(c * HALF, HALF)
    half1 = mo((1 - c) * HALF, HALF)

    def at(sec, yy, zz, cc):
        return (sec, yy * 16 + zz * 2 + cc)

    def send(src, dst, ss, rs, device):
        pltpu.make_async_remote_copy(
            src_ref=src, dst_ref=dst, send_sem=ss, recv_sem=rs, device_id=device, device_id_type=MESH
        ).start()

    small = [
        pltpu.make_async_copy(hin_hbm, hin, w_sem.at[3]),
        pltpu.make_async_copy(gain_hbm, gain, w_sem.at[4]),
        pltpu.make_async_copy(routes_hbm, routes, w_sem.at[5]),
        pltpu.make_async_copy(rweight_hbm, rweight, w_sem.at[6]),
    ]
    for copy in small:
        copy.start()
    weights = [
        pltpu.make_async_copy(wg_hbm.at[0], wg, w_sem.at[0]),
        pltpu.make_async_copy(wu_hbm.at[0], wu, w_sem.at[1]),
        pltpu.make_async_copy(wd_hbm.at[0], wd, w_sem.at[2]),
    ]
    for copy in weights:
        copy.start()

    barrier = pltpu.get_barrier_semaphore()

    def greet(device):
        pl.semaphore_signal(barrier, inc=1, device_id=device, device_id_type=MESH)

    def greet_plane(j, _):
        greet((s, plane + (q + j) % 16))
        return 0

    lax.fori_loop(1, 16, greet_plane, 0)
    for dy in (1, 2, 3):
        greet(at(s, (y + dy) % YS, z, c))

    def greet_next(j, _):
        greet(at(s + 1, y, j, c))
        return 0

    def greet_last(j, _):
        greet(at(s - 1, y, j, c))
        return 0

    @pl.when(s < SECTIONS - 1)
    def _():
        lax.fori_loop(0, ZS, greet_next, 0)

    @pl.when(s > 0)
    def _():
        lax.fori_loop(0, ZS, greet_last, 0)

    small[0].wait()
    hin_f[...] = jnp.zeros_like(hin_f)
    hin_f[0:MB, :] = hin[...].astype(F32)
    for k in range(2 * ZS):
        hin_0[k // ZS, k % ZS : k % ZS + 1, :] = hin_f[0:1, k * FB : (k + 1) * FB]

    inner = jnp.logical_and(s > 0, s < SECTIONS - 1)
    pl.semaphore_wait(barrier, jnp.where(inner, 18 + 2 * ZS, 18 + ZS))

    def ring(k):
        return (q + 8 + (1 - 2 * (k % 2)) * ((k + 1) // 2)) % 16

    @pl.when(s == 0)
    def _():
        def spread_0(k, _):
            qq = ring(k)
            send(hin_0.at[qq % 2], tin_0.at[q], tin0_s, tin0_r, (s, plane + qq))
            return 0

        lax.fori_loop(0, 15, spread_0, 0)
        pltpu.make_async_copy(hin_0.at[c], tin_0.at[q], tin0_r).start()

    for copy in small[1:]:
        copy.wait()
    expert = ep // 4
    for m in range(MB):
        rw = rweight[0, m]
        hit = jnp.sum(jnp.where(routes[0, m] == expert, rw, 0.0), axis=0, keepdims=True)
        share = hit / jnp.sum(rw, axis=0, keepdims=True)
        coeff[m] = jnp.swapaxes(jnp.broadcast_to(share, (128, ROWS)), 0, 1)
    out_t[...] = jnp.zeros_like(out_t)

    def block(m, yy, bb):
        return xg.at[m, pl.ds(mo(yy * RB, RB), RB), pl.ds(mo(bb * FB, FB), FB)]

    def phase_a(m):
        first = jnp.logical_and(s == 0, m == 0)

        @pl.when(first)
        def _():
            wait(tin_0, tin0_r)
            for k in range(ZS):
                xg[m, pl.ds(row0, RB), pl.ds(mo(half0 + k * FB, FB), FB)] = tin_0[:, k, :].astype(BF)

            def spread(k, _):
                qq = ring(k)
                bb = (qq % 2) * ZS + qq // 2
                send(hin_f.at[:, pl.ds(mo(bb * FB, FB), FB)], tin.at[q], tin_s, tin_r, (s, plane + qq))
                return 0

            lax.fori_loop(0, 15, spread, 0)
            tin[q] = hin_f[:, pl.ds(col0, FB)]

        mine = block(m, y, b)

        def gather():
            for off in FAR_FIRST:
                send(mine, mine, s_a.at[m], agz_r.at[m, z], at(s, y, (z + off) % ZS, c))

        @pl.when(jnp.logical_and(s == 0, m > 0))
        def _():
            @pl.when(m == 1)
            def _():
                wait(tin.at[pl.ds(0, 15)], tin_r)

            xg[m, pl.ds(row0, RB), pl.ds(col0, FB)] = tin[:, m, :].astype(BF)
            gather()

        @pl.when(s > 0)
        def _():
            wait(res.at[m], res_r.at[m])
            total = res[m].astype(F32)
            wait(rsz.at[m], rsz_r.at[m])
            for k in range(ZS):
                total = total + rsz[m, k].astype(F32)
            xg[m, pl.ds(row0, RB), pl.ds(col0, FB)] = total.astype(BF)
            gather()
            send(mine, oblk.at[m], s_ob.at[m], ob_r.at[m], at(s - 1, y, z, c))

        @pl.when(s < SECTIONS - 1)
        def _():
            send(mine, res.at[m], s_res.at[m], res_r.at[m], at(s + 1, y, z, c))

    def gather_cols(t, start):
        return pl.ds(mo(start + ((z // 2 + GATHER_ORDER[t]) % PIECES) * CH, CH), CH)

    def phase_b(m):
        for t in range(PIECES):
            @pl.when(jnp.logical_or(s > 0, m > 0))
            def _():
                pair = ((z // 2 + GATHER_ORDER[t]) % PIECES) * 2
                for zz in (pair + 1 - z % 2,) if t == 0 else (pair, pair + 1):
                    wait(block(m, y, c * ZS + zz), agz_r.at[m, zz])

            piece = xg.at[m, pl.ds(row0, RB), gather_cols(t, half0)]
            for dy in (2, 1, 3):
                send(piece, piece, s_b.at[m], agy_r.at[m, t], at(s, (y + dy) % YS, z, c))

    def to_partner(m, t):
        cols = gather_cols(t, half0)
        wait(xg.at[m, pl.ds(0, 3 * RB), cols], agy_r.at[m, t])
        piece = xg.at[m, :, cols]
        send(piece, piece, s_c.at[m], agc_r.at[m, t], partner)

    def products(m, cols, carry):
        g, u, ss = carry
        h = xg[m, :, cols].astype(F32)
        sq = h * h
        for j in range(CH // 128):
            ss = ss + sq[:, j * 128 : (j + 1) * 128]
        hg = (h * gain[:, cols]).astype(BF)
        g = g + jnp.dot(hg, wg[cols, :], preferred_element_type=F32)
        u = u + jnp.dot(hg, wu[cols, :], preferred_element_type=F32)
        return g, u, ss

    def from_partner(m, t, carry):
        cols = gather_cols(t, half1)
        wait(xg.at[m, :, cols], agc_r.at[m, t])
        return products(m, cols, carry)

    def start_sums():
        return jnp.zeros((ROWS, FF), F32), jnp.zeros((ROWS, FF), F32), jnp.zeros((ROWS, 128), F32)

    def activate(m, carry):
        g, u, ss = carry
        scale = lax.rsqrt(jnp.sum(ss, axis=-1, keepdims=True) * (1.0 / D) + 1e-06)
        g = g * scale
        act_s[m] = (jax.nn.silu(g) * (u * scale) * coeff[m, :, 0:1]).astype(BF)

    def phase_c(m):
        for t in range(PIECES):
            to_partner(m, t)

    def phase_d(m):
        carry = start_sums()
        for t in range(PIECES):
            carry = products(m, gather_cols(t, half0), carry)
        for t in range(PIECES):
            carry = from_partner(m, t, carry)
        activate(m, carry)

    def phase_g(m):
        for t, off in enumerate(SUM_ORDER):
            piece = (z // 2 + off) % PIECES
            src = mo((1 - c) * HALF + piece * CH, CH)
            cols = pl.ds(mo(piece * CH, CH), CH)
            pc[m, :, cols] = jnp.dot(act_s[m], wd[:, pl.ds(src, CH)], preferred_element_type=F32).astype(BF)
            send(pc.at[m, :, cols], rsc.at[m, :, cols], s_d.at[m], rsc_r.at[m, t], partner)
        for off in SUM_ORDER:
            piece = (z // 2 + off) % PIECES
            src = mo(c * HALF + piece * CH, CH)
            cols = pl.ds(mo(piece * CH, CH), CH)
            part[m, :, cols] = jnp.dot(act_s[m], wd[:, pl.ds(src, CH)], preferred_element_type=F32)

    def phase_e(m):
        for t, off in enumerate(SUM_ORDER):
            cols = pl.ds(mo(((z // 2 + off) % 4) * CH, CH), CH)
            wait(rsc.at[m, :, cols], rsc_r.at[m, t])
            py[m, :, cols] = (part[m, :, cols] + rsc[m, :, cols].astype(F32)).astype(BF)
            for dy in (2, 1, 3):
                yy = (y + dy) % YS
                send(
                    py.at[m, pl.ds(mo(yy * RB, RB), RB), cols],
                    rsy.at[m, pl.ds((dy - 1) * RB, RB), cols],
                    s_e.at[m], rsy_r.at[m, t], at(s, yy, z, c),
                )

    def phase_f(m):
        def total_of(t):
            piece = (z // GROUP + SUM_ORDER[t]) % PIECES
            cols = pl.ds(mo(piece * CH, CH), CH)
            wait(rsy.at[m, :, cols], rsy_r.at[m, t])
            total = py[m, pl.ds(row0, RB), cols].astype(F32)
            for k in range(YS - 1):
                total = total + rsy[m, k * RB : (k + 1) * RB, cols].astype(F32)
            return piece, cols, total

        @pl.when(s < SECTIONS - 1)
        def _():
            for t in range(PIECES):
                piece, cols, total = total_of(t)
                pz[m, :, cols] = total.astype(BF)
                for e in range(GROUP):
                    zz = piece * GROUP + e
                    src = pz.at[m, :, pl.ds(mo(zz * FB, FB), FB)]
                    send(src, rsz.at[m, z], s_f.at[m], rsz_r.at[m], at(s + 1, y, zz, c))

        @pl.when(s == SECTIONS - 1)
        def _():
            for t in range(PIECES):
                piece, cols, total = total_of(t)
                for e in range(GROUP):
                    pzf[m, :, piece * GROUP + e, :] = total[:, e * FB : (e + 1) * FB]

            pzf[m, :, z, :] = pzf[m, :, z, :] + xg[m, pl.ds(row0, RB), pl.ds(col0, FB)].astype(F32)

            def give(k, _):
                qq = ring(k)
                send(pzf.at[m, qq], orow_l.at[m, q], s_f.at[m], orl_r.at[m], (s, plane + qq))
                return 0

            lax.fori_loop(0, 15, give, 0)
            pltpu.make_async_copy(pzf.at[m, q], orow_l.at[m, q], orl_r.at[m]).start()

    phases = {"A": phase_a, "B": phase_b, "C": phase_c, "D": phase_d, "G": phase_g, "E": phase_e, "F": phase_f}

    def slot(n, _):
        for name, lag in SCHEDULE:
            m = n - lag

            if name == "D":
                @pl.when(m == 0)
                def _():
                    for copy in weights:
                        copy.wait()

            @pl.when(jnp.logical_and(m >= 0, m < MB))
            def _():
                phases[name](m)

        return 0

    lax.fori_loop(0, SLOTS, slot, 0)

    @pl.when(s < SECTIONS - 1)
    def _():
        for m in range(MB):
            wait(oblk.at[m], ob_r.at[m])
            out_t[:, m, :] = oblk[m].astype(F32)

        def collect(k, _):
            qq = ring(k)
            send(out_t.at[qq], orow.at[b], or_s, or_r, (s, plane + qq))
            return 0

        lax.fori_loop(0, 15, collect, 0)
        orow[b] = out_t[q]
        wait(orow.at[pl.ds(0, 15)], or_r)

    @pl.when(s == SECTIONS - 1)
    def _():
        for m in range(MB):
            wait(orow_l.at[m], orl_r.at[m])
            for cc in range(2):
                total = orow_l[m, cc]
                for k in range(1, ZS):
                    total = total + orow_l[m, 2 * k + cc]
                orow[cc * ZS : (cc + 1) * ZS, m, :] = total

    for k in range(2 * ZS):
        out[:, k * FB : (k + 1) * FB] = orow[k, 0:MB, :].astype(BF)

    @pl.when(s == 0)
    def _():
        wait(tin_0.at[pl.ds(0, 15)], tin0_s)
        wait(tin.at[pl.ds(0, 15)], tin_s)

    @pl.when(s < SECTIONS - 1)
    def _():
        wait(orow.at[pl.ds(0, 15)], or_s)

    for m in range(MB):
        def gathered(m=m):
            wait(xg.at[m, pl.ds(0, RB), pl.ds(0, 7 * FB)], s_a.at[m])

        if m:
            gathered()
        else:
            pl.when(s > 0)(gathered)
        wait(xg.at[m, pl.ds(0, 3 * RB), pl.ds(0, HALF)], s_b.at[m])
        wait(xg.at[m, :, pl.ds(0, HALF)], s_c.at[m])
        wait(pc.at[m], s_d.at[m])
        wait(rsy.at[m], s_e.at[m])

        @pl.when(s < SECTIONS - 1)
        def _():
            wait(rsz.at[m], s_f.at[m])
            wait(res.at[m], s_res.at[m])

        @pl.when(s == SECTIONS - 1)
        def _():
            wait(orow_l.at[m, pl.ds(0, 15)], s_f.at[m])

        @pl.when(s > 0)
        def _():
            wait(oblk.at[m], s_ob.at[m])


def local(hidden_in, norm_gain, gate_weight, up_weight, down_weight, routes, route_weight):
    vmem = pl.BlockSpec(memory_space=pltpu.VMEM)
    hbm = pl.BlockSpec(memory_space=pl.ANY)
    dma = pltpu.SemaphoreType.DMA
    rows = pl.pallas_call(
        kernel,
        name="moe_layers",
        out_shape=jax.ShapeDtypeStruct((MB, D), BF),
        in_specs=[hbm] * 7,
        out_specs=vmem,
        scratch_shapes=[
            pltpu.VMEM((MB, D), BF),
            pltpu.VMEM((1, D), F32),
            pltpu.VMEM((1, MB, 8, ROWS), jnp.int32),
            pltpu.VMEM((1, MB, 8, ROWS), F32),
            pltpu.VMEM((D, FF), BF),
            pltpu.VMEM((D, FF), BF),
            pltpu.VMEM((FF, D), BF),
            pltpu.VMEM((MB, ROWS, D), BF),
            pltpu.VMEM((8, D), F32),
            pltpu.VMEM((16, 8, FB), F32),
            pltpu.VMEM((MB, ROWS, 128), F32),
            pltpu.VMEM((MB, ROWS, FF), BF),
            pltpu.VMEM((MB, ROWS, HALF), BF),
            pltpu.VMEM((MB, ROWS, HALF), BF),
            pltpu.VMEM((MB, ROWS, HALF), F32),
            pltpu.VMEM((MB, ROWS, HALF), BF),
            pltpu.VMEM((MB, 3 * RB, HALF), BF),
            pltpu.VMEM((MB, RB, HALF), BF),
            pltpu.VMEM((MB, ZS, RB, FB), BF),
            pltpu.VMEM((MB, RB, FB), BF),
            pltpu.VMEM((MB, RB, FB), BF),
            pltpu.VMEM((16, 8, FB), F32),
            pltpu.VMEM((16, 8, FB), F32),
            pltpu.VMEM((2, ZS, FB), F32),
            pltpu.VMEM((16, ZS, FB), F32),
            pltpu.VMEM((MB, 16, ZS, FB), F32),
            pltpu.VMEM((MB, 16, ZS, FB), F32),
            dma((7,)),
            dma, dma,
            dma, dma,
            dma((MB,)),
            dma((MB, ZS)),
            dma((MB, PIECES)),
            dma((MB, PIECES)),
            dma((MB, 4)),
            dma((MB, 4)),
            dma((MB,)),
            dma((MB,)),
            dma((MB,)),
            dma, dma,
            dma((MB,)), dma((MB,)), dma((MB,)), dma((MB,)), dma((MB,)), dma((MB,)), dma((MB,)), dma((MB,)),
        ],
        compiler_params=pltpu.CompilerParams(
            collective_id=0, has_side_effects=True, vmem_limit_bytes=60 << 20
        ),
        cost_estimate=pl.CostEstimate(
            flops=6 * MB * ROWS * D * FF, bytes_accessed=6 * D * FF, transcendentals=MB * ROWS * FF
        ),
    )(
        hidden_in.reshape(MB, D),
        norm_gain,
        gate_weight,
        up_weight,
        down_weight,
        jnp.swapaxes(routes, 2, 3),
        jnp.swapaxes(route_weight, 2, 3),
    )
    return rows[None, :, None, :]


def solution(mesh):
    return jax.shard_map(
        local,
        mesh=mesh,
        in_specs=(
            P(None, "ep", None),
            P("section", None),
            P("section", None, "ep"),
            P("section", None, "ep"),
            P("section", "ep", None),
            P("section", None, None, None),
            P("section", None, None, None),
        ),
        out_specs=P("section", None, "ep", None),
        check_vma=False,
    )
```

```python
import functools

import jax
import jax.numpy as jnp
from jax import lax
from jax.experimental import pallas as pl
from jax.experimental.pallas import tpu as pltpu
from jax.sharding import PartitionSpec as P

MESH = pl.DeviceIdType.MESH
BF = jnp.bfloat16
F32 = jnp.float32

D = 4096
FF = 384
MB = 4
SECTIONS = 4
YS, ZS = 4, 8
ROWS = 64
RB = 16
FB = 256
HALF = D // 2
CH = 512
PIECES = HALF // CH
GROUP = CH // FB
FAR_FIRST = (4, 3, 5, 2, 6, 1, 7)
GATHER_ORDER = (0, 1, 3, 2)
SUM_ORDER = (2, 1, 3, 0)

SCHEDULE = (("A", 0), ("D", 2), ("G", 2), ("F", 3), ("E", 2), ("C", 1), ("B", 0))
SLOTS = MB + 3


def mo(value, by):
    return pl.multiple_of(value, by)


def wait(ref, sem):
    pltpu.make_async_copy(ref, ref, sem).wait()


def kernel(
    hin_hbm, gain_hbm, wg_hbm, wu_hbm, wd_hbm, routes_hbm, rweight_hbm, out,
    hin, gain, routes, rweight, wg, wu, wd, xg, hin_f, tin, coeff, act_s, pc, rsc, part, py, rsy, pz, rsz,
    res, oblk, out_t, orow, hin_0, tin_0, pzf, orow_l,
    w_sem, tin_r, tin_s, tin0_r, tin0_s, orl_r, agz_r, agy_r, agc_r, rsc_r, rsy_r, rsz_r, res_r, ob_r, or_r, or_s,
    s_a, s_res, s_ob, s_b, s_c, s_d, s_e, s_f,
):
    s = lax.axis_index("section")
    ep = lax.axis_index("ep")
    y = ep // 16
    q = ep % 16
    z = q // 2
    c = q % 2
    b = c * ZS + z
    plane = y * 16
    partner = (s, plane + z * 2 + (1 - c))
    row0 = mo(y * RB, RB)
    col0 = mo(b * FB, FB)
    half0 = mo(c * HALF, HALF)
    half1 = mo((1 - c) * HALF, HALF)

    def at(sec, yy, zz, cc):
        return (sec, yy * 16 + zz * 2 + cc)

    def send(src, dst, ss, rs, device):
        pltpu.make_async_remote_copy(
            src_ref=src, dst_ref=dst, send_sem=ss, recv_sem=rs, device_id=device, device_id_type=MESH
        ).start()

    small = [
        pltpu.make_async_copy(hin_hbm, hin, w_sem.at[3]),
        pltpu.make_async_copy(gain_hbm, gain, w_sem.at[4]),
        pltpu.make_async_copy(routes_hbm, routes, w_sem.at[5]),
        pltpu.make_async_copy(rweight_hbm, rweight, w_sem.at[6]),
    ]
    for copy in small:
        copy.start()
    weights = [
        pltpu.make_async_copy(wg_hbm.at[0], wg, w_sem.at[0]),
        pltpu.make_async_copy(wu_hbm.at[0], wu, w_sem.at[1]),
        pltpu.make_async_copy(wd_hbm.at[0], wd, w_sem.at[2]),
    ]
    for copy in weights:
        copy.start()

    barrier = pltpu.get_barrier_semaphore()

    def greet(device):
        pl.semaphore_signal(barrier, inc=1, device_id=device, device_id_type=MESH)

    def greet_plane(j, _):
        greet((s, plane + (q + j) % 16))
        return 0

    lax.fori_loop(1, 16, greet_plane, 0)
    for dy in (1, 2, 3):
        greet(at(s, (y + dy) % YS, z, c))

    def greet_next(j, _):
        greet(at(s + 1, y, j, c))
        return 0

    def greet_last(j, _):
        greet(at(s - 1, y, j, c))
        return 0

    @pl.when(s < SECTIONS - 1)
    def _():
        lax.fori_loop(0, ZS, greet_next, 0)

    @pl.when(s > 0)
    def _():
        lax.fori_loop(0, ZS, greet_last, 0)

    small[0].wait()
    hin_f[...] = jnp.zeros_like(hin_f)
    hin_f[0:MB, :] = hin[...].astype(F32)
    for k in range(2 * ZS):
        hin_0[k // ZS, k % ZS : k % ZS + 1, :] = hin_f[0:1, k * FB : (k + 1) * FB]

    inner = jnp.logical_and(s > 0, s < SECTIONS - 1)
    pl.semaphore_wait(barrier, jnp.where(inner, 18 + 2 * ZS, 18 + ZS))

    def ring(k):
        return (q + 8 + (1 - 2 * (k % 2)) * ((k + 1) // 2)) % 16

    @pl.when(s == 0)
    def _():
        def spread_0(k, _):
            qq = ring(k)
            send(hin_0.at[qq % 2], tin_0.at[q], tin0_s, tin0_r, (s, plane + qq))
            return 0

        lax.fori_loop(0, 15, spread_0, 0)
        pltpu.make_async_copy(hin_0.at[c], tin_0.at[q], tin0_r).start()

    for copy in small[1:]:
        copy.wait()
    expert = ep // 4
    for m in range(MB):
        rw = rweight[0, m]
        hit = jnp.sum(jnp.where(routes[0, m] == expert, rw, 0.0), axis=0, keepdims=True)
        share = hit / jnp.sum(rw, axis=0, keepdims=True)
        coeff[m] = jnp.swapaxes(jnp.broadcast_to(share, (128, ROWS)), 0, 1)
    out_t[...] = jnp.zeros_like(out_t)

    def block(m, yy, bb):
        return xg.at[m, pl.ds(mo(yy * RB, RB), RB), pl.ds(mo(bb * FB, FB), FB)]

    def phase_a(m):
        first = jnp.logical_and(s == 0, jnp.bool_(m == 0))

        @pl.when(first)
        def _():
            wait(tin_0, tin0_r)
            for k in range(ZS):
                xg[m, pl.ds(row0, RB), pl.ds(mo(half0 + k * FB, FB), FB)] = tin_0[:, k, :].astype(BF)

            def spread(k, _):
                qq = ring(k)
                bb = (qq % 2) * ZS + qq // 2
                send(hin_f.at[:, pl.ds(mo(bb * FB, FB), FB)], tin.at[q], tin_s, tin_r, (s, plane + qq))
                return 0

            lax.fori_loop(0, 15, spread, 0)
            tin[q] = hin_f[:, pl.ds(col0, FB)]

        mine = block(m, y, b)

        def gather():
            for off in FAR_FIRST:
                send(mine, mine, s_a.at[m], agz_r.at[m, z], at(s, y, (z + off) % ZS, c))

        @pl.when(jnp.logical_and(s == 0, jnp.bool_(m > 0)))
        def _():
            @pl.when(jnp.bool_(m == 1))
            def _():
                wait(tin.at[pl.ds(0, 15)], tin_r)

            xg[m, pl.ds(row0, RB), pl.ds(col0, FB)] = tin[:, m, :].astype(BF)
            gather()

        @pl.when(s > 0)
        def _():
            wait(res.at[m], res_r.at[m])
            total = res[m].astype(F32)
            wait(rsz.at[m], rsz_r.at[m])
            for k in range(ZS):
                total = total + rsz[m, k].astype(F32)
            xg[m, pl.ds(row0, RB), pl.ds(col0, FB)] = total.astype(BF)
            gather()
            send(mine, oblk.at[m], s_ob.at[m], ob_r.at[m], at(s - 1, y, z, c))

        @pl.when(s < SECTIONS - 1)
        def _():
            send(mine, res.at[m], s_res.at[m], res_r.at[m], at(s + 1, y, z, c))

    def gather_cols(t, start):
        return pl.ds(mo(start + ((z // 2 + GATHER_ORDER[t]) % PIECES) * CH, CH), CH)

    def phase_b(m):
        for t in range(PIECES):
            @pl.when(jnp.logical_or(s > 0, jnp.bool_(m > 0)))
            def _():
                pair = ((z // 2 + GATHER_ORDER[t]) % PIECES) * 2
                for zz in (pair + 1 - z % 2,) if t == 0 else (pair, pair + 1):
                    wait(block(m, y, c * ZS + zz), agz_r.at[m, zz])

            piece = xg.at[m, pl.ds(row0, RB), gather_cols(t, half0)]
            for dy in (2, 1, 3):
                send(piece, piece, s_b.at[m], agy_r.at[m, t], at(s, (y + dy) % YS, z, c))

    def to_partner(m, t):
        cols = gather_cols(t, half0)
        wait(xg.at[m, pl.ds(0, 3 * RB), cols], agy_r.at[m, t])
        piece = xg.at[m, :, cols]
        send(piece, piece, s_c.at[m], agc_r.at[m, t], partner)

    def products(m, cols, carry):
        g, u, ss = carry
        h = xg[m, :, cols].astype(F32)
        sq = h * h
        for j in range(CH // 128):
            ss = ss + sq[:, j * 128 : (j + 1) * 128]
        hg = (h * gain[:, cols]).astype(BF)
        g = g + jnp.dot(hg, wg[cols, :], preferred_element_type=F32)
        u = u + jnp.dot(hg, wu[cols, :], preferred_element_type=F32)
        return g, u, ss

    def from_partner(m, t, carry):
        cols = gather_cols(t, half1)
        wait(xg.at[m, :, cols], agc_r.at[m, t])
        return products(m, cols, carry)

    def start_sums():
        return jnp.zeros((ROWS, FF), F32), jnp.zeros((ROWS, FF), F32), jnp.zeros((ROWS, 128), F32)

    def activate(m, carry):
        g, u, ss = carry
        scale = lax.rsqrt(jnp.sum(ss, axis=-1, keepdims=True) * (1.0 / D) + 1e-06)
        g = g * scale
        act_s[m] = (jax.nn.silu(g) * (u * scale) * coeff[m, :, 0:1]).astype(BF)

    def phase_c(m):
        for t in range(PIECES):
            to_partner(m, t)

    def phase_d(m):
        carry = start_sums()
        for t in range(PIECES):
            carry = products(m, gather_cols(t, half0), carry)
        for t in range(PIECES):
            carry = from_partner(m, t, carry)
        activate(m, carry)

    def phase_g(m):
        for t, off in enumerate(SUM_ORDER):
            piece = (z // 2 + off) % PIECES
            src = mo((1 - c) * HALF + piece * CH, CH)
            cols = pl.ds(mo(piece * CH, CH), CH)
            pc[m, :, cols] = jnp.dot(act_s[m], wd[:, pl.ds(src, CH)], preferred_element_type=F32).astype(BF)
            send(pc.at[m, :, cols], rsc.at[m, :, cols], s_d.at[m], rsc_r.at[m, t], partner)
        for off in SUM_ORDER:
            piece = (z // 2 + off) % PIECES
            src = mo(c * HALF + piece * CH, CH)
            cols = pl.ds(mo(piece * CH, CH), CH)
            part[m, :, cols] = jnp.dot(act_s[m], wd[:, pl.ds(src, CH)], preferred_element_type=F32)

    def phase_e(m):
        for t, off in enumerate(SUM_ORDER):
            cols = pl.ds(mo(((z // 2 + off) % 4) * CH, CH), CH)
            wait(rsc.at[m, :, cols], rsc_r.at[m, t])
            py[m, :, cols] = (part[m, :, cols] + rsc[m, :, cols].astype(F32)).astype(BF)
            for dy in (2, 1, 3):
                yy = (y + dy) % YS
                send(
                    py.at[m, pl.ds(mo(yy * RB, RB), RB), cols],
                    rsy.at[m, pl.ds((dy - 1) * RB, RB), cols],
                    s_e.at[m], rsy_r.at[m, t], at(s, yy, z, c),
                )

    def phase_f(m):
        def total_of(t):
            piece = (z // GROUP + SUM_ORDER[t]) % PIECES
            cols = pl.ds(mo(piece * CH, CH), CH)
            wait(rsy.at[m, :, cols], rsy_r.at[m, t])
            total = py[m, pl.ds(row0, RB), cols].astype(F32)
            for k in range(YS - 1):
                total = total + rsy[m, k * RB : (k + 1) * RB, cols].astype(F32)
            return piece, cols, total

        @pl.when(s < SECTIONS - 1)
        def _():
            for t in range(PIECES):
                piece, cols, total = total_of(t)
                pz[m, :, cols] = total.astype(BF)
                for e in range(GROUP):
                    zz = piece * GROUP + e
                    src = pz.at[m, :, pl.ds(mo(zz * FB, FB), FB)]
                    send(src, rsz.at[m, z], s_f.at[m], rsz_r.at[m], at(s + 1, y, zz, c))

        @pl.when(s == SECTIONS - 1)
        def _():
            for t in range(PIECES):
                piece, cols, total = total_of(t)
                for e in range(GROUP):
                    pzf[m, :, piece * GROUP + e, :] = total[:, e * FB : (e + 1) * FB]

            pzf[m, :, z, :] = pzf[m, :, z, :] + xg[m, pl.ds(row0, RB), pl.ds(col0, FB)].astype(F32)

            def give(k, _):
                qq = ring(k)
                send(pzf.at[m, qq], orow_l.at[m, q], s_f.at[m], orl_r.at[m], (s, plane + qq))
                return 0

            lax.fori_loop(0, 15, give, 0)
            pltpu.make_async_copy(pzf.at[m, q], orow_l.at[m, q], orl_r.at[m]).start()

    phases = {"A": phase_a, "B": phase_b, "C": phase_c, "D": phase_d, "G": phase_g, "E": phase_e, "F": phase_f}

    steps = [(name, n - lag) for n in range(SLOTS) for name, lag in SCHEDULE if 0 <= n - lag < MB]
    for name, m in steps:
        if (name, m) == ("D", 0):
            for copy in weights:
                copy.wait()
        phases[name](m)

    @pl.when(s < SECTIONS - 1)
    def _():
        for m in range(MB):
            wait(oblk.at[m], ob_r.at[m])
            out_t[:, m, :] = oblk[m].astype(F32)

        def collect(k, _):
            qq = ring(k)
            send(out_t.at[qq], orow.at[b], or_s, or_r, (s, plane + qq))
            return 0

        lax.fori_loop(0, 15, collect, 0)
        orow[b] = out_t[q]
        wait(orow.at[pl.ds(0, 15)], or_r)

    @pl.when(s == SECTIONS - 1)
    def _():
        for m in range(MB):
            wait(orow_l.at[m], orl_r.at[m])
            for cc in range(2):
                total = orow_l[m, cc]
                for k in range(1, ZS):
                    total = total + orow_l[m, 2 * k + cc]
                orow[cc * ZS : (cc + 1) * ZS, m, :] = total

    for k in range(2 * ZS):
        out[:, k * FB : (k + 1) * FB] = orow[k, 0:MB, :].astype(BF)

    @pl.when(s == 0)
    def _():
        wait(tin_0.at[pl.ds(0, 15)], tin0_s)
        wait(tin.at[pl.ds(0, 15)], tin_s)

    @pl.when(s < SECTIONS - 1)
    def _():
        wait(orow.at[pl.ds(0, 15)], or_s)

    for m in range(MB):
        def gathered(m=m):
            wait(xg.at[m, pl.ds(0, RB), pl.ds(0, 7 * FB)], s_a.at[m])

        if m:
            gathered()
        else:
            pl.when(s > 0)(gathered)
        wait(xg.at[m, pl.ds(0, 3 * RB), pl.ds(0, HALF)], s_b.at[m])
        wait(xg.at[m, :, pl.ds(0, HALF)], s_c.at[m])
        wait(pc.at[m], s_d.at[m])
        wait(rsy.at[m], s_e.at[m])

        @pl.when(s < SECTIONS - 1)
        def _():
            wait(rsz.at[m], s_f.at[m])
            wait(res.at[m], s_res.at[m])

        @pl.when(s == SECTIONS - 1)
        def _():
            wait(orow_l.at[m, pl.ds(0, 15)], s_f.at[m])

        @pl.when(s > 0)
        def _():
            wait(oblk.at[m], s_ob.at[m])


def local(hidden_in, norm_gain, gate_weight, up_weight, down_weight, routes, route_weight):
    vmem = pl.BlockSpec(memory_space=pltpu.VMEM)
    hbm = pl.BlockSpec(memory_space=pl.ANY)
    dma = pltpu.SemaphoreType.DMA
    rows = pl.pallas_call(
        kernel,
        name="moe_layers",
        out_shape=jax.ShapeDtypeStruct((MB, D), BF),
        in_specs=[hbm] * 7,
        out_specs=vmem,
        scratch_shapes=[
            pltpu.VMEM((MB, D), BF),
            pltpu.VMEM((1, D), F32),
            pltpu.VMEM((1, MB, 8, ROWS), jnp.int32),
            pltpu.VMEM((1, MB, 8, ROWS), F32),
            pltpu.VMEM((D, FF), BF),
            pltpu.VMEM((D, FF), BF),
            pltpu.VMEM((FF, D), BF),
            pltpu.VMEM((MB, ROWS, D), BF),
            pltpu.VMEM((8, D), F32),
            pltpu.VMEM((16, 8, FB), F32),
            pltpu.VMEM((MB, ROWS, 128), F32),
            pltpu.VMEM((MB, ROWS, FF), BF),
            pltpu.VMEM((MB, ROWS, HALF), BF),
            pltpu.VMEM((MB, ROWS, HALF), BF),
            pltpu.VMEM((MB, ROWS, HALF), F32),
            pltpu.VMEM((MB, ROWS, HALF), BF),
            pltpu.VMEM((MB, 3 * RB, HALF), BF),
            pltpu.VMEM((MB, RB, HALF), BF),
            pltpu.VMEM((MB, ZS, RB, FB), BF),
            pltpu.VMEM((MB, RB, FB), BF),
            pltpu.VMEM((MB, RB, FB), BF),
            pltpu.VMEM((16, 8, FB), F32),
            pltpu.VMEM((16, 8, FB), F32),
            pltpu.VMEM((2, ZS, FB), F32),
            pltpu.VMEM((16, ZS, FB), F32),
            pltpu.VMEM((MB, 16, ZS, FB), F32),
            pltpu.VMEM((MB, 16, ZS, FB), F32),
            dma((7,)),
            dma, dma,
            dma, dma,
            dma((MB,)),
            dma((MB, ZS)),
            dma((MB, PIECES)),
            dma((MB, PIECES)),
            dma((MB, 4)),
            dma((MB, 4)),
            dma((MB,)),
            dma((MB,)),
            dma((MB,)),
            dma, dma,
            dma((MB,)), dma((MB,)), dma((MB,)), dma((MB,)), dma((MB,)), dma((MB,)), dma((MB,)), dma((MB,)),
        ],
        compiler_params=pltpu.CompilerParams(
            collective_id=0, has_side_effects=True, vmem_limit_bytes=60 << 20
        ),
        cost_estimate=pl.CostEstimate(
            flops=6 * MB * ROWS * D * FF, bytes_accessed=6 * D * FF, transcendentals=MB * ROWS * FF
        ),
    )(
        hidden_in.reshape(MB, D),
        norm_gain,
        gate_weight,
        up_weight,
        down_weight,
        jnp.swapaxes(routes, 2, 3),
        jnp.swapaxes(route_weight, 2, 3),
    )
    return rows[None, :, None, :]


def solution(mesh):
    return jax.shard_map(
        local,
        mesh=mesh,
        in_specs=(
            P(None, "ep", None),
            P("section", None),
            P("section", None, "ep"),
            P("section", None, "ep"),
            P("section", "ep", None),
            P("section", None, None, None),
            P("section", None, None, None),
        ),
        out_specs=P("section", None, "ep", None),
        check_vma=False,
    )
```
